128 devices in a mesh: front: 8 (over z, core), helper: 16 (over x, y).
Axes of the slice: x: 4, y: 4, z: 4, core: 2. Of those that a mesh axis runs over, the one named last changes fastest.
Arguments:
- front: float32 [8, 4096, 4096], P('front', 'helper')
- row_list: int32 [8, 4096], replicated, may hold values from 0 to 4095, as said below
- child_map: int32 [8, 3840], replicated, may hold values from 0 to 8191, as said below
- parent: float32 [8192, 8192], P(('front', 'helper')), may hold values from -6 to 6
Outputs:
- factors: float32 [8, 4096, 4096], P('front', 'helper')
- assembled: float32 [8192, 8192], P(('front', 'helper'))
The draws below stay inside these ranges and needn't reach their ends.
Inputs may be any that keep to these rules, and one draw needn't show every extreme that they name: Each row of row_list is a permutation; stored rows h * 256 to (h + 1) * 256 - 1 of a front lie on helper h. Of the 256 rows of any panel, one helper holds at most 24, and some helper holds exactly 24 in every panel. The leading 256 x 256 block of every front is well conditioned without pivoting: its diagonal exceeds 2.5 sqrt(256) times the row's spread. `child_map`: distinct within a front. Parent row r lies on device r // 64 of front+helper. Of the contribution rows on one device, at most 2 go to one device's parent rows, and exactly 2 go to some device.
All inputs are finite; a program needn't handle non-finite values.
Results may differ from the reference program's by a relative error of at most 0.0001.
Values sent between devices are 32-bit elements; how exact they have to be, the bound alone decides.
No kernel may reach another device: no remote copies, remote signals or barrier semaphores. Data moves between devices by JAX's collectives and lax.ppermute only.
A program may use at most 128 MiB of HBM per device.

```python
import jax
import jax.numpy as jnp
from jax import lax

FRONT_ORDER = 4096
PANEL = 256
PANELS = 1
PARENT_ORDER = 8192
FRONTS = 8
ROWS_DEV = 256
PIVOTS = 256
CB_ORDER = 3840
XCAP = 2
PARENT_ROWS = 64


def one_front(front_key, base_counts):
    helpers = FRONT_ORDER // ROWS_DEV
    devices_all = FRONTS * helpers
    blocks_each = (ROWS_DEV + XCAP - 1) // XCAP
    key_list = jax.random.split(front_key, 6)
    helper_perms = jax.vmap(lambda sub: jax.random.permutation(sub, helpers))(jax.random.split(key_list[0], PANELS))
    counts = base_counts[helper_perms].T
    bounds = jnp.concatenate([jnp.zeros((helpers, 1), jnp.int32), jnp.cumsum(counts, axis=1)], axis=1)
    slot_iota = jnp.arange(ROWS_DEV, dtype=jnp.int32)
    labels = jnp.sum((slot_iota[None, :, None] >= bounds[:, None, 1:]).astype(jnp.int32), axis=2)
    within = slot_iota[None, :] - jnp.take_along_axis(bounds, labels, axis=1)
    offsets = jnp.cumsum(counts, axis=0) - counts
    safe_labels = jnp.minimum(labels, PANELS - 1)
    panel_slot = jnp.take_along_axis(offsets, safe_labels, axis=1) + within
    panel_perms = jax.vmap(lambda sub: jax.random.permutation(sub, PANEL))(jax.random.split(key_list[1], PANELS))
    panel_rows = safe_labels * PANEL + panel_perms[safe_labels, jnp.clip(panel_slot, 0, PANEL - 1)]
    cb_count = ROWS_DEV - bounds[:, PANELS]
    cb_offsets = jnp.cumsum(cb_count) - cb_count
    cb_perm = jax.random.permutation(key_list[2], CB_ORDER)
    cb_slot = jnp.clip(cb_offsets[:, None] + within, 0, CB_ORDER - 1)
    cb_rows = PIVOTS + cb_perm[cb_slot]
    is_cb = labels == PANELS
    row_ids = jnp.where(is_cb, cb_rows, panel_rows)
    owner_perm = jax.random.permutation(key_list[3], devices_all)
    block_index = jnp.clip(within // XCAP, 0, blocks_each - 1)
    pick_index = jnp.arange(helpers, dtype=jnp.int32)[:, None] * blocks_each + block_index
    owners = owner_perm[pick_index % devices_all]
    arrival = pick_index // devices_all * XCAP + within % XCAP
    slot_perms = jax.vmap(lambda sub: jax.random.permutation(sub, PARENT_ROWS))(jax.random.split(key_list[4], devices_all))
    targets = owners * PARENT_ROWS + slot_perms[owners, jnp.clip(arrival, 0, PARENT_ROWS - 1)]
    place = jnp.where(is_cb, row_ids - PIVOTS, CB_ORDER).reshape(-1)
    parent_map = jnp.zeros((CB_ORDER,), jnp.int32).at[place].set(targets.reshape(-1).astype(jnp.int32), mode='drop')
    shuffle = jax.vmap(lambda sub: jax.random.permutation(sub, ROWS_DEV))(jax.random.split(key_list[5], helpers))
    stored = jnp.take_along_axis(row_ids, shuffle, axis=1).reshape(FRONT_ORDER)
    return (stored.astype(jnp.int32), parent_map)


def layout(key):
    helpers = FRONT_ORDER // ROWS_DEV
    per_helper = PANEL // helpers
    half_count = helpers // 2
    helper_iota = jnp.arange(helpers, dtype=jnp.int32)
    mirror = jnp.minimum(helper_iota, helpers - 1 - helper_iota)
    swing = per_helper // 2 * (half_count - mirror) // max(half_count, 1)
    base_counts = jnp.where(helper_iota < half_count, per_helper + swing, per_helper - swing).astype(jnp.int32)
    front_keys = jax.random.split(key, FRONTS)
    return jax.vmap(lambda sub: one_front(sub, base_counts))(front_keys)


def draw_row_list(key, part):
    stored, parent_map = layout(key)
    return stored


def draw_child_map(key, part):
    stored, parent_map = layout(key)
    return parent_map


def draw_front(key, part):
    stored, parent_map = layout(key)
    key = jax.random.fold_in(key, 3)
    value_key, diag_key = jax.random.split(key, 2)
    shape = (FRONTS, FRONT_ORDER, FRONT_ORDER)
    values = jnp.clip(jax.random.normal(value_key, shape, jnp.float32), -6.0, 6.0)
    diagonal = PIVOTS ** 0.5 * jax.random.uniform(diag_key, (FRONTS, FRONT_ORDER, 1), jnp.float32, 2.5, 4.0)
    columns = jnp.arange(FRONT_ORDER, dtype=jnp.int32)
    full = jnp.where(columns[None, None, :] == stored[:, :, None], diagonal, values)
    return full.astype(jnp.float32)


def shard_levels(rng, dims, cuts, least, high):
    gain = 1.0
    for position, parts in cuts:
        heights = jax.random.uniform(jax.random.fold_in(jax.random.fold_in(rng, 6), position), (parts,), jnp.float32, least / len(cuts), high / len(cuts))
        gain = gain * jnp.repeat(jnp.exp(heights), dims[position] // parts).reshape((-1,) + (1,) * (len(dims) - 1 - position))
    return gain


def bell_draw(own_key, shape, deviation, limit, shards=(), kind=jnp.bfloat16):
    array = deviation * jax.random.normal(own_key, shape, jnp.float32)
    if shards:
        array = array * shard_levels(own_key, shape, shards, -0.22, 0.18)
    return jnp.clip(array, -limit, limit).astype(kind)


def setup_inputs(seed: int = 0) -> dict:
    keys = jax.random.split(jax.random.key(seed), 5)
    return {
        "front": draw_front(jax.random.fold_in(keys[4], 71), 0),
        "row_list": draw_row_list(jax.random.fold_in(keys[4], 71), 0),
        "child_map": draw_child_map(jax.random.fold_in(keys[4], 71), 0),
        "parent": bell_draw(keys[3], (PARENT_ORDER, PARENT_ORDER), 1.0, 6.0, ((0, 128),), jnp.float32),
    }


def product(left, right):
    return jnp.dot(left, right, precision=lax.Precision.HIGHEST, preferred_element_type=jnp.float32)


def small_inverse(matrix):
    extent = matrix.shape[0]
    augmented = jnp.concatenate([matrix, jnp.eye(extent, dtype=matrix.dtype)], axis=1)
    for column in range(extent):
        pivot_row = augmented[column] / augmented[column, column]
        augmented = augmented - augmented[:, column:column + 1] * pivot_row[None, :]
        augmented = augmented.at[column].set(pivot_row)
    return augmented[:, extent:]


def block_inverse(matrix):
    extent = matrix.shape[0]
    if extent <= 32:
        return small_inverse(matrix)
    middle = extent // 2
    upper_left = matrix[:middle, :middle]
    upper_right = matrix[:middle, middle:]
    lower_left = matrix[middle:, :middle]
    lower_right = matrix[middle:, middle:]
    inverse_left = block_inverse(upper_left)
    coupled = product(inverse_left, upper_right)
    schur_part = lower_right - product(lower_left, coupled)
    inverse_schur = block_inverse(schur_part)
    left_factor = product(lower_left, inverse_left)
    top_right = -product(coupled, inverse_schur)
    bottom_left = -product(inverse_schur, left_factor)
    top_left = inverse_left - product(top_right, left_factor)
    upper_half = jnp.concatenate([top_left, top_right], axis=1)
    lower_half = jnp.concatenate([bottom_left, inverse_schur], axis=1)
    return jnp.concatenate([upper_half, lower_half], axis=0)


def eliminate(stored, row_order):
    natural = jnp.zeros_like(stored).at[row_order].set(stored)
    for panel_index in range(PANELS):
        first_col = panel_index * PANEL
        end_col = first_col + PANEL
        inverse = block_inverse(natural[first_col:end_col, first_col:end_col])
        lower_part = product(natural[end_col:, first_col:end_col], inverse)
        natural = natural.at[end_col:, first_col:end_col].set(lower_part)
        natural = natural.at[end_col:, end_col:].add(-product(lower_part, natural[first_col:end_col, end_col:]))
    return natural[row_order], natural[PIVOTS:, PIVOTS:]


def reference(front, row_list, child_map, parent):
    assembled = parent
    factor_list = []
    for front_index in range(FRONTS):
        done, contribution = eliminate(front[front_index], row_list[front_index])
        factor_list.append(done)
        targets = child_map[front_index]
        assembled = assembled.at[targets[:, None], targets[None, :]].add(contribution)
    return jnp.stack(factor_list), assembled
```

```python
import jax
import jax.numpy as jnp
from jax import lax
from jax.experimental import pallas as pl
from jax.experimental.pallas import tpu as pltpu
from jax.sharding import PartitionSpec as P

PIVOTS = 256
CAP = 24
BASE = 32
F32 = jnp.float32
BF16 = jnp.bfloat16
I32 = jnp.int32
GRID = 4
X_UP, X_DOWN, Y_UP, Y_DOWN = (1, 0), (3, 0), (0, 1), (0, 3)
BIG = pltpu.CompilerParams(vmem_limit_bytes=58 << 20)


def iota(shape, axis):
    return lax.broadcasted_iota(I32, shape, axis)


def exact(left, right):
    return jnp.dot(left, right, precision=lax.Precision.HIGHEST, preferred_element_type=F32)


def halves(value):
    high = value.astype(BF16)
    return high, (value - high.astype(F32)).astype(BF16)


def dot16(left, right):
    return jnp.dot(left, right, preferred_element_type=F32)


def dot3(left, right):
    left_high, left_low = halves(left)
    right_high, right_low = halves(right)
    return dot16(left_high, right_high) + (dot16(left_high, right_low) + dot16(left_low, right_high))


def select_kernel(ids_ref, front_ref, pivot_ref, first_ref, second_ref):
    rows = front_ref.shape[0]
    half = first_ref.shape[1]
    ids = ids_ref[...]
    inside = jnp.broadcast_to((ids < PIVOTS).astype(F32), (8, rows)).astype(BF16)
    before = (iota((rows, rows), 0) < iota((rows, rows), 1)).astype(F32).astype(BF16)
    rank = dot16(inside, before)[:1].astype(I32)
    rank = jnp.where(ids < PIVOTS, rank, -1)
    chosen = (jnp.broadcast_to(rank, (CAP, rows)) == iota((CAP, rows), 0)).astype(F32)
    pivot_ref[...] = exact(chosen, front_ref[:, :PIVOTS])
    step = 384
    for start in range(0, half, step):
        first_ref[:, start : start + step] = exact(chosen, front_ref[:, PIVOTS + start : PIVOTS + start + step])
        at = PIVOTS + half + start
        second_ref[:, start : start + step] = exact(chosen, front_ref[:, at : at + step])


def select_panel(own_ids, front_rows):
    half = (front_rows.shape[1] - PIVOTS) // 2
    return pl.pallas_call(
        select_kernel,
        out_shape=(
            jax.ShapeDtypeStruct((CAP, PIVOTS), F32),
            jax.ShapeDtypeStruct((CAP, half), F32),
            jax.ShapeDtypeStruct((CAP, half), F32),
        ),
        compiler_params=BIG,
    )(own_ids[None, :], front_rows)


def shift_pairs(step):
    return [
        (x * GRID + y, (x + step[0]) % GRID * GRID + (y + step[1]) % GRID)
        for x in range(GRID)
        for y in range(GRID)
    ]


def shift(value, step):
    return lax.ppermute(value, "helper", shift_pairs(step))


def spread_panel(first, second):
    cut = 16
    first_up, first_down = shift(first, X_UP), shift(first, X_DOWN)
    second_up, second_down = shift(second, Y_UP), shift(second, Y_DOWN)
    first_far = shift(first_up[:cut], X_UP), shift(first_down[cut:], X_DOWN)
    second_far = shift(second_up[:cut], Y_UP), shift(second_down[cut:], Y_DOWN)
    line = jnp.concatenate([first, first_up, first_down, *first_far])
    file = jnp.concatenate([second, second_up, second_down, *second_far])
    middle = 2 * CAP
    line_up, line_down = shift(line, Y_UP), shift(line, Y_DOWN)
    file_up, file_down = shift(file, X_UP), shift(file, X_DOWN)
    line_far = shift(line_up[:middle], Y_UP), shift(line_down[middle:], Y_DOWN)
    file_far = shift(file_up[:middle], X_UP), shift(file_down[middle:], X_DOWN)
    return (line, line_up, line_down, *line_far), (file, file_up, file_down, *file_far)


def inverse_kernel(slot_abs_ref, slot_rel_ref, piv_ref, inv_ref, inv_rel_ref):
    slots = piv_ref.shape[0]
    natural = (iota((PIVOTS, slots), 0) == slot_abs_ref[...]).astype(F32)
    inv_ref[...] = exact(natural, piv_ref[...])
    lanes = iota((1, PIVOTS), 1)
    for block in range(PIVOTS // BASE):
        base = block * BASE
        rows = inv_ref[base : base + BASE, :]
        sub = iota((BASE, 1), 0)
        for step in range(BASE):
            at = base + step
            here = lanes == at
            pivot_row = rows[step : step + 1, :]
            scaled = jnp.where(here, 1.0, pivot_row) / pivot_row[:, at : at + 1]
            column = rows[:, at : at + 1]
            rows = jnp.where(sub == step, scaled, jnp.where(here, 0.0, rows) - column * scaled)
        in_block = (lanes >= base) & (lanes < base + BASE)
        full = inv_ref[...]
        left = jnp.where(in_block, full, 0.0)
        kept = jnp.where(in_block, 0.0, full)
        parts = []
        if base:
            parts.append(jnp.zeros((base, PIVOTS), F32))
        parts.append(rows)
        if base + BASE < PIVOTS:
            parts.append(jnp.zeros((PIVOTS - base - BASE, PIVOTS), F32))
        inv_ref[...] = kept - exact(left, jnp.concatenate(parts, axis=0))
        inv_ref[base : base + BASE, :] = rows
    relative = (iota((PIVOTS, slots), 0) == slot_rel_ref[...]).astype(F32)
    inv_rel_ref[...] = exact(inv_ref[...], relative)


def invert(slot_abs, slot_rel, piv):
    slots = piv.shape[0]
    return pl.pallas_call(
        inverse_kernel,
        out_shape=(
            jax.ShapeDtypeStruct((PIVOTS, PIVOTS), F32),
            jax.ShapeDtypeStruct((PIVOTS, slots), F32),
        ),
        compiler_params=BIG,
    )(slot_abs, slot_rel, piv)


OFFSETS = (0, 3, 1, 2)


def eliminate_kernel(
    active_ref, place_ref, rank_ref, inv_ref, inv_rel_ref, front_ref, *refs
):
    first_refs, second_refs = refs[:5], refs[5:10]
    factors_ref, send_ref, upper, sorted_in = refs[10:]
    rows = front_ref.shape[0]
    width = front_ref.shape[1] - PIVOTS
    half = width // 2
    for piece in range(4):
        for block in range(4):
            into = (block * 4 + piece) * CAP
            if piece < 3:
                upper[into : into + CAP, :half] = first_refs[piece][block * CAP : (block + 1) * CAP, :]
            else:
                at = block % 2 * CAP
                upper[into : into + CAP, :half] = first_refs[3 + block // 2][at : at + CAP, :]
            into = (piece * 4 + block) * CAP
            if piece < 3:
                upper[into : into + CAP, half:] = second_refs[piece][block * CAP : (block + 1) * CAP, :]
            else:
                at = block % 2 * CAP
                upper[into : into + CAP, half:] = second_refs[3 + block // 2][at : at + CAP, :]
    active = active_ref[...] > 0
    current = front_ref[:, :PIVOTS]
    factors_ref[:, :PIVOTS] = jnp.where(active, dot3(current, inv_ref[...]), current)
    lower = jnp.where(active, dot3(current, inv_rel_ref[...]), 0.0)
    lower_high, lower_low = halves(lower)
    place = (iota((rows, rows), 0) == place_ref[...]).astype(F32).astype(BF16)
    tile = 256

    def update(index, carry):
        at = pl.multiple_of(index * tile, tile)
        high, low = halves(upper[:, pl.ds(at, tile)])
        change = dot16(lower_high, high) + (dot16(lower_high, low) + dot16(lower_low, high))
        out = front_ref[:, pl.ds(at + PIVOTS, tile)] - change
        factors_ref[:, pl.ds(at + PIVOTS, tile)] = out
        high, low = halves(out)
        sorted_in[:rows, pl.ds(at, tile)] = dot16(place, high).astype(BF16)
        sorted_in[rows:, pl.ds(at, tile)] = dot16(place, low).astype(BF16)
        return carry

    lax.fori_loop(0, width // tile, update, 0)

    def permute(index, carry):
        at = pl.multiple_of(index * tile, tile)
        lane = iota((1, 128), 1) + at
        ranks = rank_ref[...]
        moves = jnp.concatenate([(ranks == lane), (ranks == lane + 128)], axis=1).astype(F32).astype(BF16)
        out = dot16(sorted_in[...], moves)
        send_ref[:, pl.ds(at, tile)] = out[:rows] + out[rows:]
        return carry

    lax.fori_loop(0, width // tile, permute, 0)


def eliminate(active, place, rank, inv, inv_rel, front_rows, line, file):
    rows, columns = front_rows.shape
    width = columns - PIVOTS
    return pl.pallas_call(
        eliminate_kernel,
        out_shape=(
            jax.ShapeDtypeStruct((rows, columns), F32),
            jax.ShapeDtypeStruct((rows, width), F32),
        ),
        scratch_shapes=[
            pltpu.VMEM((16 * CAP, width), F32),
            pltpu.VMEM((2 * rows, width), BF16),
        ],
        compiler_params=BIG,
    )(active, place, rank, inv, inv_rel, front_rows, *line, *file)


def assemble_kernel(group_ref, source_ref, put_ref, received_ref, parent_ref, out_ref):
    fronts = source_ref.shape[0]
    per_front = received_ref.shape[0] // fronts
    last = received_ref.shape[1] // 128 - 1
    step = pl.program_id(0)
    tile = out_ref.shape[1]
    columns = []
    for part in range(tile // 128):
        pieces = []
        for front in range(fronts):
            group = jnp.minimum(group_ref[front, step * (tile // 128) + part], last)
            following = jnp.minimum(group + 1, last)
            source = source_ref[front : front + 1, part * 128 : (part + 1) * 128]
            lane = jnp.broadcast_to(source & 127, (per_front, 128))
            which = source >> 7
            span = pl.ds(front * per_front, per_front)
            near = received_ref[span, pl.ds(pl.multiple_of(group * 128, 128), 128)]
            far = received_ref[span, pl.ds(pl.multiple_of(following * 128, 128), 128)]
            near = jnp.take_along_axis(near, lane, axis=1)
            far = jnp.take_along_axis(far, lane, axis=1)
            pieces.append(jnp.where(which == group, near, jnp.where(which == following, far, 0.0)))
        columns.append(jnp.concatenate(pieces, axis=0))
    spread = jnp.concatenate(columns, axis=1)
    high, low = halves(spread)
    put = put_ref[...]
    out_ref[...] = parent_ref[...] + (dot16(put, high) + dot16(put, low))


def assemble(group, source, put, received, parent):
    rows, width = parent.shape
    fronts = source.shape[0]
    tile = 256
    return pl.pallas_call(
        assemble_kernel,
        grid_spec=pltpu.PrefetchScalarGridSpec(
            num_scalar_prefetch=1,
            grid=(width // tile,),
            in_specs=[
                pl.BlockSpec((fronts, tile), lambda i, g: (0, i)),
                pl.BlockSpec(put.shape, lambda i, g: (0, 0)),
                pl.BlockSpec(received.shape, lambda i, g: (0, 0)),
                pl.BlockSpec((rows, tile), lambda i, g: (0, i)),
            ],
            out_specs=pl.BlockSpec((rows, tile), lambda i, g: (0, i)),
        ),
        out_shape=jax.ShapeDtypeStruct((rows, width), F32),
        compiler_params=BIG,
    )(group, source, put, received, parent)


def local(front, row_list, child_map, parent):
    front_rows = front[0]
    rows = front_rows.shape[0]
    width = front_rows.shape[1] - PIVOTS
    helpers = lax.axis_size("helper")
    fronts = lax.axis_size("front")
    devices = helpers * fronts
    cap = (rows + devices - 1) // devices
    parent_rows, parent_width = parent.shape
    my_front = lax.axis_index("front")
    my_helper = lax.axis_index("helper")
    me = my_front * helpers + my_helper
    order = jnp.take(row_list, my_front, axis=0)
    by_helper = order.reshape(helpers, rows)
    own_ids = lax.dynamic_slice_in_dim(order, my_helper * rows, rows)

    pivot, first, second = select_panel(own_ids, front_rows)
    piv = lax.all_gather(pivot, "helper", axis=0, tiled=True)
    line, file = spread_panel(first, second)

    inside = by_helper < PIVOTS
    earlier = (jnp.arange(rows)[:, None] < jnp.arange(rows)[None, :]).astype(BF16)
    slot_rank = dot16(inside.astype(BF16), earlier).astype(I32)
    slot_iota = jnp.arange(CAP, dtype=I32)
    hit = (slot_rank[:, None, :] == slot_iota[None, :, None]) & inside[:, None, :]
    slot_row = jnp.sum(jnp.where(hit, by_helper[:, None, :] + 1, 0), axis=2) - 1
    grid_iota = jnp.array(OFFSETS, I32)
    source_x = (my_helper // GRID + grid_iota) % GRID
    source_y = (my_helper % GRID + grid_iota) % GRID
    relative = (source_x[:, None] * GRID + source_y[None, :]).reshape(helpers)
    slot_rel = jnp.sum(
        jnp.where((relative[:, None] == jnp.arange(helpers)[None, :])[:, :, None], slot_row[None], 0), axis=1
    )
    inv, inv_rel = invert(slot_row.reshape(1, -1), slot_rel.reshape(1, -1), piv)

    own_map = jnp.take(child_map, my_front, axis=0)
    own_cb = own_ids >= PIVOTS
    column_iota = jnp.arange(width, dtype=I32)
    own_target = jnp.sum(
        jnp.where((own_ids - PIVOTS)[:, None] == column_iota[None, :], own_map[None, :], 0), axis=1
    )
    owner = jnp.where(own_cb, own_target // parent_rows, -1)
    row_iota = jnp.arange(rows, dtype=I32)
    same = (owner[:, None] == owner[None, :]) & (row_iota[None, :] < row_iota[:, None])
    place = jnp.where(own_cb, owner * cap + jnp.sum(same.astype(I32), axis=1), -1)

    high_iota = jnp.arange(parent_width // 128, dtype=I32)
    low_iota = jnp.arange(128, dtype=I32)
    in_high = ((child_map >> 7)[:, :, None] == high_iota).astype(BF16)
    in_low = ((child_map & 127)[:, :, None] == low_iota).astype(BF16)
    counts = jnp.einsum("fah,fal->fhl", in_high, in_low, preferred_element_type=F32)
    within = jnp.einsum(
        "fhl,lm->fhm",
        counts.astype(BF16),
        (low_iota[:, None] < low_iota[None, :]).astype(BF16),
        preferred_element_type=F32,
    )
    totals = jnp.sum(counts, axis=2)
    starts = jnp.einsum(
        "fh,hg->fg",
        totals.astype(BF16),
        (high_iota[:, None] < high_iota[None, :]).astype(BF16),
        preferred_element_type=F32,
    )
    below = starts[:, :, None] + within
    source = jnp.where(counts > 0, below, -1.0).astype(I32).reshape(fronts, parent_width)
    group = starts.astype(I32) >> 7
    own_below = jnp.take(below, my_front, axis=0)
    own_high = ((own_map >> 7)[:, None] == high_iota).astype(F32)
    rank = jnp.sum(
        jnp.where((own_map & 127)[:, None] == low_iota, exact(own_high, own_below), 0.0), axis=1
    ).astype(I32)
    rank = jnp.broadcast_to(rank[:, None], (width, 128))

    factors, outgoing = eliminate(
        own_cb[:, None].astype(I32), place[None, :], rank, inv, inv_rel, front_rows, line, file
    )
    received = lax.all_to_all(
        outgoing.reshape(devices, cap, width), ("front", "helper"), split_axis=0, concat_axis=0, tiled=True
    ).reshape(devices * cap, width)

    own_parent = me * parent_rows + jnp.arange(parent_rows, dtype=I32)
    column = jnp.sum(
        jnp.where(child_map[:, None, :] == own_parent[None, :, None], column_iota + 1, 0), axis=2
    )
    found = column > 0
    stored = jnp.sum(
        jnp.where(
            row_list[:, None, :] == (column + (PIVOTS - 1))[:, :, None],
            jnp.arange(row_list.shape[1], dtype=I32),
            0,
        ),
        axis=2,
    )
    sender = stored // rows
    ahead = jnp.sum(
        (
            found[:, None, :]
            & (sender[:, :, None] == sender[:, None, :])
            & (stored[:, None, :] < stored[:, :, None])
        ).astype(I32),
        axis=2,
    )
    front_iota = jnp.arange(fronts, dtype=I32)
    slot = jnp.where(found, (front_iota[:, None] * helpers + sender) * cap + ahead, -1)
    put = jnp.any(slot[:, :, None] == jnp.arange(devices * cap, dtype=I32), axis=0).astype(BF16)
    assembled = assemble(group, source, put, received, parent)
    return (factors[None], assembled)


def solution(mesh):
    in_specs = (P("front", "helper", None), P(), P(), P(("front", "helper"), None))
    out_specs = (P("front", "helper", None), P(("front", "helper"), None))
    return jax.shard_map(local, mesh=mesh, in_specs=in_specs, out_specs=out_specs, check_vma=False)
```

```python
import jax
import jax.numpy as jnp
from jax import lax
from jax.experimental import pallas as pl
from jax.experimental.pallas import tpu as pltpu
from jax.sharding import PartitionSpec as P

PIVOTS = 256
CAP = 24
BASE = 32
F32 = jnp.float32
BF16 = jnp.bfloat16
I32 = jnp.int32
GRID = 4
X_UP, X_DOWN, X_FAR = (1, 0), (3, 0), (2, 0)
Y_UP, Y_DOWN, Y_FAR = (0, 1), (0, 3), (0, 2)
BIG = pltpu.CompilerParams(vmem_limit_bytes=58 << 20)


def iota(shape, axis):
    return lax.broadcasted_iota(I32, shape, axis)


def exact(left, right):
    return jnp.dot(left, right, precision=lax.Precision.HIGHEST, preferred_element_type=F32)


def halves(value):
    high = value.astype(BF16)
    return high, (value - high.astype(F32)).astype(BF16)


def dot16(left, right):
    return jnp.dot(left, right, preferred_element_type=F32)


def dot3(left, right):
    left_high, left_low = halves(left)
    right_high, right_low = halves(right)
    return dot16(left_high, right_high) + (dot16(left_high, right_low) + dot16(left_low, right_high))


def select_kernel(ids_ref, front_ref, pivot_ref, first_ref, second_ref):
    rows = front_ref.shape[0]
    ids = ids_ref[...]
    inside = jnp.broadcast_to((ids < PIVOTS).astype(F32), (8, rows)).astype(BF16)
    before = (iota((rows, rows), 0) < iota((rows, rows), 1)).astype(F32).astype(BF16)
    rank = dot16(inside, before)[:1].astype(I32)
    rank = jnp.where(ids < PIVOTS, rank, -1)
    chosen = (jnp.broadcast_to(rank, (CAP, rows)) == iota((CAP, rows), 0)).astype(F32).astype(BF16)

    def pick(start, into):
        step = 512
        for at in range(0, into.shape[1], step):
            stop = min(at + step, into.shape[1])
            value = front_ref[:, start + at : start + stop]
            high = value.astype(BF16)
            middle, low = halves(value - high.astype(F32))
            into[:, at:stop] = dot16(chosen, high) + (dot16(chosen, middle) + dot16(chosen, low))

    pick(0, pivot_ref)
    pick(PIVOTS, first_ref)
    pick(PIVOTS + first_ref.shape[1], second_ref)


def select_panel(own_ids, front_rows):
    half = (front_rows.shape[1] - PIVOTS) // 2
    return pl.pallas_call(
        select_kernel,
        out_shape=(
            jax.ShapeDtypeStruct((CAP, PIVOTS), F32),
            jax.ShapeDtypeStruct((CAP, half), F32),
            jax.ShapeDtypeStruct((CAP, half), F32),
        ),
        compiler_params=BIG,
    )(own_ids[None, :], front_rows)


def shift_pairs(step):
    return [
        (x * GRID + y, (x + step[0]) % GRID * GRID + (y + step[1]) % GRID)
        for x in range(GRID)
        for y in range(GRID)
    ]


def shift(value, step):
    return lax.ppermute(value, "helper", shift_pairs(step))


def pack_kernel(*refs):
    for index in range(8):
        into = slice(index % 2 * CAP, (index % 2 + 1) * CAP)
        refs[8 + index // 2][into, :] = refs[index][...]


def pack(firsts, seconds):
    half = seconds[0].shape[1]
    return pl.pallas_call(
        pack_kernel,
        out_shape=(jax.ShapeDtypeStruct((2 * CAP, half), F32),) * 4,
        compiler_params=BIG,
    )(*firsts, *seconds)


def rank_kernel(map_ref, rank_ref):
    width = map_ref.shape[1]
    high = (iota((64, width), 0) == (map_ref[...] >> 7)).astype(F32).astype(BF16)
    in_low = iota((128, width), 0) == (map_ref[...] & 127)
    low = in_low.astype(F32).astype(BF16)
    counts = lax.dot_general(high, low, (((1,), (1,)), ((), ())), preferred_element_type=F32)
    before = (iota((128, 128), 0) < iota((128, 128), 1)).astype(F32).astype(BF16)
    within = dot16(counts.astype(BF16), before)
    earlier = (iota((64, 64), 1) < iota((64, 64), 0)).astype(F32).astype(BF16)
    starts = jnp.sum(dot16(earlier, counts.astype(BF16)), axis=1, keepdims=True)
    below = (starts + within).astype(I32)
    coarse = (below >> 6).astype(F32).astype(BF16)
    fine = (below & 63).astype(F32).astype(BF16)
    contract = (((0,), (0,)), ((), ()))
    table = 64.0 * lax.dot_general(coarse, high, contract, preferred_element_type=F32)
    table = table + lax.dot_general(fine, high, contract, preferred_element_type=F32)
    row = jnp.sum(jnp.where(in_low, table, 0.0), axis=0, keepdims=True)
    for start in range(0, width, 128):
        block = jnp.broadcast_to(row[:, start : start + 128], (128, 128))
        rank_ref[start : start + 128, :] = block.T.astype(I32)


def column_ranks(own_map):
    width = own_map.shape[0]
    return pl.pallas_call(
        rank_kernel, out_shape=jax.ShapeDtypeStruct((width, 128), I32), compiler_params=BIG
    )(own_map[None, :])


def inverse_kernel(slot_abs_ref, slot_rel_ref, piv_ref, inv_ref, inv_rel_ref):
    slots = piv_ref.shape[0]
    natural = (iota((PIVOTS, slots), 0) == slot_abs_ref[...]).astype(F32)
    inv_ref[...] = exact(natural, piv_ref[...])
    lanes = iota((1, PIVOTS), 1)
    for block in range(PIVOTS // BASE):
        base = block * BASE
        rows = inv_ref[base : base + BASE, :]
        sub = iota((BASE, 1), 0)
        for step in range(BASE):
            at = base + step
            here = lanes == at
            pivot_row = rows[step : step + 1, :]
            if step == 0:
                column = jnp.broadcast_to(rows[:, at : at + 1], (BASE, 128))
                following = jnp.broadcast_to(rows[:, at + 1 : at + 2], (BASE, 128))
            recip = 1.0 / column[step : step + 1, :]
            if step + 2 < BASE:
                ahead = jnp.broadcast_to(rows[:, at + 2 : at + 3], (BASE, 128))
            scaled = jnp.where(here, 1.0, pivot_row) * jnp.concatenate([recip, recip], axis=1)
            both = jnp.concatenate([column, column], axis=1)
            rows = jnp.where(sub == step, scaled, jnp.where(here, 0.0, rows) - both * scaled)

            def turn(value):
                turned = value[step : step + 1, :] * recip
                return jnp.where(sub == step, turned, value - column * turned)

            if step + 1 < BASE:
                turned_next = turn(following)
                if step + 2 < BASE:
                    following = turn(ahead)
                column = turned_next
        in_block = (lanes >= base) & (lanes < base + BASE)
        full = inv_ref[...]
        left = jnp.where(in_block, full, 0.0)
        kept = jnp.where(in_block, 0.0, full)
        parts = []
        if base:
            parts.append(jnp.zeros((base, PIVOTS), F32))
        parts.append(rows)
        if base + BASE < PIVOTS:
            parts.append(jnp.zeros((PIVOTS - base - BASE, PIVOTS), F32))
        inv_ref[...] = kept - exact(left, jnp.concatenate(parts, axis=0))
        inv_ref[base : base + BASE, :] = rows
    relative = (iota((PIVOTS, slots), 0) == slot_rel_ref[...]).astype(F32)
    inv_rel_ref[...] = exact(inv_ref[...], relative)


def invert(slot_abs, slot_rel, piv):
    slots = piv.shape[0]
    return pl.pallas_call(
        inverse_kernel,
        out_shape=(
            jax.ShapeDtypeStruct((PIVOTS, PIVOTS), F32),
            jax.ShapeDtypeStruct((PIVOTS, slots), F32),
        ),
        compiler_params=BIG,
    )(slot_abs, slot_rel, piv)


OFFSETS = (0, 3, 1, 2)


def eliminate_kernel(
    active_ref, place_ref, inv_ref, inv_rel_ref, rank_hbm, front_hbm, *refs
):
    pieces, refs = refs[:16], refs[16:]
    factors_hbm, send_hbm = refs[:2]
    matrix, upper, ranks, sorted_in, moves, send = refs[2:8]
    front_sem, upper_sem, rank_sem, factors_sem, send_sem = refs[8:]
    rows, columns = matrix.shape
    width = columns - PIVOTS
    half = width // 2
    tile = 256
    tiles = width // tile

    loads = [pltpu.make_async_copy(front_hbm.at[:, :PIVOTS], matrix.at[:, :PIVOTS], front_sem.at[0])]
    for part in range(2):
        at = PIVOTS + part * half
        loads.append(
            pltpu.make_async_copy(front_hbm.at[:, at : at + half], matrix.at[:, at : at + half], front_sem.at[part + 1])
        )
    rank_load = pltpu.make_async_copy(rank_hbm, ranks, rank_sem)
    upper_loads = []
    for part in range(2):
        into = slice(part * half, (part + 1) * half)
        for piece in range(4):
            for block in range(4):
                source, at = pieces[part * 8 + piece * 2 + block // 2], block % 2 * CAP
                slot = ((block * 4 + piece) if part == 0 else (piece * 4 + block)) * CAP
                upper_loads.append(
                    pltpu.make_async_copy(
                        source.at[at : at + CAP, :], upper.at[slot : slot + CAP, into], upper_sem.at[part * 16 + piece * 4 + block]
                    )
                )
    loads[0].start()
    loads[1].start()
    for load in upper_loads[:16]:
        load.start()
    loads[2].start()
    for load in upper_loads[16:]:
        load.start()
    rank_load.start()

    loads[0].wait()
    active = active_ref[...] > 0
    current = matrix[:, :PIVOTS]
    lower = jnp.where(active, dot3(current, inv_rel_ref[...]), 0.0)
    lower_high, lower_low = halves(lower)
    lower_both = jnp.concatenate([lower_high, lower_low], axis=0)
    matrix[:, :PIVOTS] = jnp.where(active, dot3(current, inv_ref[...]), current)
    stores = [pltpu.make_async_copy(matrix.at[:, :PIVOTS], factors_hbm.at[:, :PIVOTS], factors_sem.at[0])]
    stores[0].start()
    place = (iota((rows, rows), 0) == place_ref[...]).astype(F32).astype(BF16)

    def update(at, size):
        high, low = halves(upper[:, pl.ds(at, size)])
        change = dot16(lower_both, high)
        change = change[:rows] + (change[rows:] + dot16(lower_high, low))
        out = matrix[:, pl.ds(at + PIVOTS, size)] - change
        matrix[:, pl.ds(at + PIVOTS, size)] = out
        high, low = halves(out)
        placed = dot16(place, jnp.concatenate([high, low], axis=1)).astype(BF16)
        sorted_in[:rows, pl.ds(at, size)] = placed[:, :size]
        sorted_in[rows:, pl.ds(at, size)] = placed[:, size:]

    def generate(slot, index):
        lane = iota((1, 128), 1) + index * tile
        for part in range(2):
            moves[slot, :, part * 128 : (part + 1) * 128] = (
                (ranks[...] == lane + part * 128).astype(F32).astype(BF16)
            )

    for part in range(2):
        loads[part + 1].wait()
        for load in upper_loads[part * 16 : part * 16 + 16]:
            load.wait()

        def updates(index, carry):
            update(pl.multiple_of(part * half + index * 384, 128), 384)
            return carry

        lax.fori_loop(0, half // 384, updates, 0)
        at = PIVOTS + part * half
        stores.append(
            pltpu.make_async_copy(matrix.at[:, at : at + half], factors_hbm.at[:, at : at + half], factors_sem.at[part + 1])
        )
        stores[-1].start()

    rank_load.wait()
    generate(0, 0)

    def permute(slot, index):
        at = pl.multiple_of(index * tile, tile)
        out = dot16(sorted_in[...], moves[slot])
        send[:, :, pl.ds(at, tile)] = (out[:rows] + out[rows:]).reshape(rows // 2, 2, tile)
        pltpu.make_async_copy(
            send.at[:, :, pl.ds(at, tile)], send_hbm.at[:, :, pl.ds(at, tile)], send_sem.at[index]
        ).start()

    def pair(index, carry):
        generate(1, 2 * index + 1)
        permute(0, 2 * index)
        generate(0, 2 * index + 2)
        permute(1, 2 * index + 1)
        return carry

    lax.fori_loop(0, tiles // 2, pair, 0)
    permute(0, tiles - 1)
    for store in stores:
        store.wait()
    for index in range(tiles):
        at = index * tile
        pltpu.make_async_copy(
            send.at[:, :, at : at + tile], send_hbm.at[:, :, at : at + tile], send_sem.at[index]
        ).wait()


def eliminate(active, place, rank, inv, inv_rel, front_rows, line, file):
    rows, columns = front_rows.shape
    width = columns - PIVOTS
    vmem = pl.BlockSpec(memory_space=pltpu.VMEM)
    hbm = pl.BlockSpec(memory_space=pl.ANY)
    return pl.pallas_call(
        eliminate_kernel,
        in_specs=[vmem] * 4 + [hbm] * 18,
        out_specs=(hbm, hbm),
        out_shape=(
            jax.ShapeDtypeStruct((rows, columns), F32),
            jax.ShapeDtypeStruct((rows // 2, 2, width), F32),
        ),
        scratch_shapes=[
            pltpu.VMEM((rows, columns), F32),
            pltpu.VMEM((16 * CAP, width), F32),
            pltpu.VMEM(rank.shape, I32),
            pltpu.VMEM((2 * rows, width), BF16),
            pltpu.VMEM((2, width, 256), BF16),
            pltpu.VMEM((rows // 2, 2, width), F32),
            pltpu.SemaphoreType.DMA((3,)),
            pltpu.SemaphoreType.DMA((32,)),
            pltpu.SemaphoreType.DMA,
            pltpu.SemaphoreType.DMA((3,)),
            pltpu.SemaphoreType.DMA((width // 256,)),
        ],
        compiler_params=BIG,
    )(active, place, inv, inv_rel, rank, front_rows, *line, *file)


def assemble_kernel(group_ref, source_ref, put_ref, received_ref, parent_ref, out_ref):
    fronts = source_ref.shape[0]
    senders = received_ref.shape[0] // fronts
    per_front = senders * received_ref.shape[1]
    last = received_ref.shape[2] // 128 - 1
    first = pl.program_id(0) * (out_ref.shape[1] // 128)
    put = put_ref[...]
    for tile in range(out_ref.shape[1] // 256):
        columns = []
        for part in (2 * tile, 2 * tile + 1):
            pieces = []
            for front in range(fronts):
                group = jnp.minimum(group_ref[front, first + part], last)
                following = jnp.minimum(group + 1, last)
                source = source_ref[front : front + 1, part * 128 : (part + 1) * 128]
                lane = jnp.broadcast_to(source & 127, (per_front, 128))
                which = source >> 7
                span = slice(front * senders, (front + 1) * senders)
                near = received_ref[span, :, pl.ds(pl.multiple_of(group * 128, 128), 128)].reshape(per_front, 128)
                far = received_ref[span, :, pl.ds(pl.multiple_of(following * 128, 128), 128)].reshape(per_front, 128)
                near = jnp.take_along_axis(near, lane, axis=1)
                far = jnp.take_along_axis(far, lane, axis=1)
                pieces.append(jnp.where(which == group, near, jnp.where(which == following, far, 0.0)))
            columns.append(jnp.concatenate(pieces, axis=0))
        high, low = halves(jnp.concatenate(columns, axis=1))
        at = slice(tile * 256, (tile + 1) * 256)
        out_ref[:, at] = parent_ref[:, at] + (dot16(put, high) + dot16(put, low))


def assemble(group, source, put, received, parent):
    rows, width = parent.shape
    fronts = source.shape[0]
    tile = 2048
    return pl.pallas_call(
        assemble_kernel,
        grid_spec=pltpu.PrefetchScalarGridSpec(
            num_scalar_prefetch=1,
            grid=(width // tile,),
            in_specs=[
                pl.BlockSpec((fronts, tile), lambda i, g: (0, i)),
                pl.BlockSpec(put.shape, lambda i, g: (0, 0)),
                pl.BlockSpec(received.shape, lambda i, g: (0, 0, 0)),
                pl.BlockSpec((rows, tile), lambda i, g: (0, i)),
            ],
            out_specs=pl.BlockSpec((rows, tile), lambda i, g: (0, i)),
        ),
        out_shape=jax.ShapeDtypeStruct((rows, width), F32),
        compiler_params=BIG,
    )(group, source, put, received, parent)


def columns_below(child_map, parent_width):
    high_iota = jnp.arange(parent_width // 128, dtype=I32)
    low_iota = jnp.arange(128, dtype=I32)
    in_high = ((child_map >> 7)[:, :, None] == high_iota).astype(BF16)
    in_low = ((child_map & 127)[:, :, None] == low_iota).astype(BF16)
    counts = jnp.einsum("fah,fal->fhl", in_high, in_low, preferred_element_type=F32)
    within = jnp.einsum(
        "fhl,lm->fhm",
        counts.astype(BF16),
        (low_iota[:, None] < low_iota[None, :]).astype(BF16),
        preferred_element_type=F32,
    )
    starts = jnp.einsum(
        "fh,hg->fg",
        jnp.sum(counts, axis=2).astype(BF16),
        (high_iota[:, None] < high_iota[None, :]).astype(BF16),
        preferred_element_type=F32,
    )
    return starts[:, :, None] + within, counts


def local(front, row_list, child_map, parent):
    front_rows = front[0]
    rows = front_rows.shape[0]
    width = front_rows.shape[1] - PIVOTS
    helpers = lax.axis_size("helper")
    fronts = lax.axis_size("front")
    devices = helpers * fronts
    cap = (rows + devices - 1) // devices
    parent_rows, parent_width = parent.shape
    my_front = lax.axis_index("front")
    my_helper = lax.axis_index("helper")
    me = my_front * helpers + my_helper
    order = jnp.take(row_list, my_front, axis=0)
    by_helper = order.reshape(helpers, rows)
    own_ids = lax.dynamic_slice_in_dim(order, my_helper * rows, rows)

    pivot, first, second = select_panel(own_ids, front_rows)
    own_map = jnp.take(child_map, my_front, axis=0)
    piv = lax.all_to_all(
        jnp.broadcast_to(pivot[None], (helpers, CAP, PIVOTS)), "helper", split_axis=0, concat_axis=0, tiled=True
    ).reshape(helpers * CAP, PIVOTS)
    firsts = (first, shift(first, X_UP), shift(first, X_DOWN), shift(first, X_FAR))
    seconds = (second, shift(second, Y_UP), shift(second, Y_DOWN), shift(second, Y_FAR))

    inside = by_helper < PIVOTS
    earlier = (jnp.arange(rows)[:, None] < jnp.arange(rows)[None, :]).astype(BF16)
    slot_rank = dot16(inside.astype(BF16), earlier).astype(I32)
    slot_iota = jnp.arange(CAP, dtype=I32)
    hit = (slot_rank[:, None, :] == slot_iota[None, :, None]) & inside[:, None, :]
    slot_row = jnp.sum(jnp.where(hit, by_helper[:, None, :] + 1, 0), axis=2) - 1
    grid_iota = jnp.array(OFFSETS, I32)
    source_x = (my_helper // GRID + grid_iota) % GRID
    source_y = (my_helper % GRID + grid_iota) % GRID
    relative = (source_x[:, None] * GRID + source_y[None, :]).reshape(helpers)
    slot_rel = jnp.sum(
        jnp.where((relative[:, None] == jnp.arange(helpers)[None, :])[:, :, None], slot_row[None], 0), axis=1
    )
    rank = column_ranks(own_map)
    slot_row, slot_rel = slot_row.reshape(1, -1), slot_rel.reshape(1, -1)
    firsts, seconds, rank, slot_row, slot_rel = lax.optimization_barrier((firsts, seconds, rank, slot_row, slot_rel))

    line_a, line_b, file_a, file_b = pack(firsts, seconds)
    line_up, line_down = shift(line_a, Y_UP), shift(line_b, Y_DOWN)
    file_up, file_down = shift(file_a, X_UP), shift(file_b, X_DOWN)
    line_rest = shift(line_b, Y_UP), shift(line_a, Y_DOWN)
    file_rest = shift(file_b, X_UP), shift(file_a, X_DOWN)
    inv, inv_rel = invert(slot_row, slot_rel, piv)
    line_up, line_down, file_up, file_down, inv, inv_rel = lax.optimization_barrier(
        (line_up, line_down, file_up, file_down, inv, inv_rel)
    )
    line = (line_a, line_b, line_up, line_rest[0], line_rest[1], line_down, shift(line_up, Y_UP), shift(line_down, Y_DOWN))
    file = (file_a, file_b, file_up, file_rest[0], file_rest[1], file_down, shift(file_up, X_UP), shift(file_down, X_DOWN))

    own_cb = own_ids >= PIVOTS
    column_iota = jnp.arange(width, dtype=I32)
    own_target = jnp.sum(
        jnp.where((own_ids - PIVOTS)[:, None] == column_iota[None, :], own_map[None, :], 0), axis=1
    )
    owner = jnp.where(own_cb, own_target // parent_rows, -1)
    row_iota = jnp.arange(rows, dtype=I32)
    same = (owner[:, None] == owner[None, :]) & (row_iota[None, :] < row_iota[:, None])
    place = jnp.where(own_cb, owner * cap + jnp.sum(same.astype(I32), axis=1), -1)

    factors, outgoing = eliminate(
        own_cb[:, None].astype(I32), place[None, :], rank, inv, inv_rel, front_rows, line, file
    )
    received = lax.all_to_all(outgoing, ("front", "helper"), split_axis=0, concat_axis=0, tiled=True)

    below, counts = columns_below(child_map, parent_width)
    source = jnp.where(counts > 0, below, -1.0).astype(I32).reshape(fronts, parent_width)
    group = below[:, :, 0].astype(I32) >> 7

    own_parent = me * parent_rows + jnp.arange(parent_rows, dtype=I32)
    column = jnp.sum(
        jnp.where(child_map[:, None, :] == own_parent[None, :, None], column_iota + 1, 0), axis=2
    )
    found = column > 0
    stored = jnp.sum(
        jnp.where(
            row_list[:, None, :] == (column + (PIVOTS - 1))[:, :, None],
            jnp.arange(row_list.shape[1], dtype=I32),
            0,
        ),
        axis=2,
    )
    sender = stored // rows
    ahead = jnp.sum(
        (
            found[:, None, :]
            & (sender[:, :, None] == sender[:, None, :])
            & (stored[:, None, :] < stored[:, :, None])
        ).astype(I32),
        axis=2,
    )
    front_iota = jnp.arange(fronts, dtype=I32)
    slot = jnp.where(found, (front_iota[:, None] * helpers + sender) * cap + ahead, -1)
    put = jnp.any(slot[:, :, None] == jnp.arange(devices * cap, dtype=I32), axis=0).astype(BF16)
    assembled = assemble(group, source, put, received, parent)
    return (factors[None], assembled)


def solution(mesh):
    in_specs = (P("front", "helper", None), P(), P(), P(("front", "helper"), None))
    out_specs = (P("front", "helper", None), P(("front", "helper"), None))
    return jax.shard_map(local, mesh=mesh, in_specs=in_specs, out_specs=out_specs, check_vma=False)
```

```python
import jax
import jax.numpy as jnp
from jax import lax
from jax.experimental import pallas as pl
from jax.experimental.pallas import tpu as pltpu
from jax.sharding import PartitionSpec as P

PIVOTS = 256
CAP = 24
BASE = 32
F32 = jnp.float32
BF16 = jnp.bfloat16
I32 = jnp.int32
GRID = 4
X_UP, X_DOWN, X_FAR = (1, 0), (3, 0), (2, 0)
Y_UP, Y_DOWN, Y_FAR = (0, 1), (0, 3), (0, 2)
BIG = pltpu.CompilerParams(vmem_limit_bytes=58 << 20)


def iota(shape, axis):
    return lax.broadcasted_iota(I32, shape, axis)


def exact(left, right):
    return jnp.dot(left, right, precision=lax.Precision.HIGHEST, preferred_element_type=F32)


def halves(value):
    high = value.astype(BF16)
    return high, (value - high.astype(F32)).astype(BF16)


def dot16(left, right):
    return jnp.dot(left, right, preferred_element_type=F32)


def dot3(left, right):
    left_high, left_low = halves(left)
    right_high, right_low = halves(right)
    return dot16(left_high, right_high) + (dot16(left_high, right_low) + dot16(left_low, right_high))


def select_kernel(ids_ref, front_ref, pivot_ref, first_ref, second_ref):
    rows = front_ref.shape[0]
    ids = ids_ref[...]
    inside = jnp.broadcast_to((ids < PIVOTS).astype(F32), (8, rows)).astype(BF16)
    before = (iota((rows, rows), 0) < iota((rows, rows), 1)).astype(F32).astype(BF16)
    rank = dot16(inside, before)[:1].astype(I32)
    rank = jnp.where(ids < PIVOTS, rank, -1)
    chosen = (jnp.broadcast_to(rank, (CAP, rows)) == iota((CAP, rows), 0)).astype(F32).astype(BF16)

    def pick(start, into):
        step = 512
        for at in range(0, into.shape[1], step):
            stop = min(at + step, into.shape[1])
            value = front_ref[:, start + at : start + stop]
            high = value.astype(BF16)
            middle, low = halves(value - high.astype(F32))
            into[:, at:stop] = dot16(chosen, high) + (dot16(chosen, middle) + dot16(chosen, low))

    high = front_ref[:, :PIVOTS].astype(BF16)
    middle, low = halves(front_ref[:, :PIVOTS] - high.astype(F32))
    pivot = dot16(chosen, high) + (dot16(chosen, middle) + dot16(chosen, low))
    for helper in range(pivot_ref.shape[0]):
        pivot_ref[helper] = pivot
    pick(PIVOTS, first_ref)
    pick(PIVOTS + first_ref.shape[1], second_ref)


def select_panel(own_ids, front_rows):
    half = (front_rows.shape[1] - PIVOTS) // 2
    return pl.pallas_call(
        select_kernel,
        out_shape=(
            jax.ShapeDtypeStruct((GRID * GRID, CAP, PIVOTS), F32),
            jax.ShapeDtypeStruct((CAP, half), F32),
            jax.ShapeDtypeStruct((CAP, half), F32),
        ),
        compiler_params=BIG,
    )(own_ids[None, :], front_rows)


def shift_pairs(step):
    return [
        (x * GRID + y, (x + step[0]) % GRID * GRID + (y + step[1]) % GRID)
        for x in range(GRID)
        for y in range(GRID)
    ]


def shift(value, step):
    return lax.ppermute(value, "helper", shift_pairs(step))


def pack_kernel(*refs):
    for index in range(8):
        into = slice(index % 4 * CAP, (index % 4 + 1) * CAP)
        refs[8 + index // 4][into, :] = refs[index][...]


def pack(firsts, seconds):
    half = seconds[0].shape[1]
    return pl.pallas_call(
        pack_kernel,
        out_shape=(jax.ShapeDtypeStruct((4 * CAP, half), F32),) * 2,
        compiler_params=BIG,
    )(*firsts, *seconds)


def cut_kernel(*refs):
    for index in range(4):
        refs[4 + index][...] = refs[index][...]


def cut(*blocks):
    rows, width = blocks[0].shape
    half = (rows // 2, width)
    return pl.pallas_call(
        cut_kernel,
        grid=(1,),
        in_specs=[pl.BlockSpec(half, lambda i: (0, 0)), pl.BlockSpec(half, lambda i: (1, 0))] * 2,
        out_specs=[pl.BlockSpec(half, lambda i: (0, 0))] * 4,
        out_shape=(jax.ShapeDtypeStruct(half, F32),) * 4,
        compiler_params=BIG,
    )(*blocks)


def rank_kernel(map_ref, rank_ref):
    width = map_ref.shape[1]
    high = (iota((64, width), 0) == (map_ref[...] >> 7)).astype(F32).astype(BF16)
    in_low = iota((128, width), 0) == (map_ref[...] & 127)
    low = in_low.astype(F32).astype(BF16)
    counts = lax.dot_general(high, low, (((1,), (1,)), ((), ())), preferred_element_type=F32)
    before = (iota((128, 128), 0) < iota((128, 128), 1)).astype(F32).astype(BF16)
    within = dot16(counts.astype(BF16), before)
    earlier = (iota((64, 64), 1) < iota((64, 64), 0)).astype(F32).astype(BF16)
    starts = jnp.sum(dot16(earlier, counts.astype(BF16)), axis=1, keepdims=True)
    below = (starts + within).astype(I32)
    coarse = (below >> 6).astype(F32).astype(BF16)
    fine = (below & 63).astype(F32).astype(BF16)
    contract = (((0,), (0,)), ((), ()))
    table = 64.0 * lax.dot_general(coarse, high, contract, preferred_element_type=F32)
    table = table + lax.dot_general(fine, high, contract, preferred_element_type=F32)
    row = jnp.sum(jnp.where(in_low, table, 0.0), axis=0, keepdims=True)
    for start in range(0, width, 128):
        block = jnp.broadcast_to(row[:, start : start + 128], (128, 128))
        rank_ref[start : start + 128, :] = block.T.astype(I32)


def column_ranks(own_map):
    width = own_map.shape[0]
    return pl.pallas_call(
        rank_kernel, out_shape=jax.ShapeDtypeStruct((width, 128), I32), compiler_params=BIG
    )(own_map[None, :])


def inverse_kernel(slot_abs_ref, slot_rel_ref, piv_ref, inv_ref, inv_rel_ref):
    slots = piv_ref.shape[0]
    natural = (iota((PIVOTS, slots), 0) == slot_abs_ref[...]).astype(F32)
    inv_ref[...] = exact(natural, piv_ref[...])
    lanes = iota((1, PIVOTS), 1)
    for block in range(PIVOTS // BASE):
        base = block * BASE
        rows = inv_ref[base : base + BASE, :]
        sub = iota((BASE, 1), 0)
        for step in range(BASE):
            at = base + step
            here = lanes == at
            pivot_row = rows[step : step + 1, :]
            if step == 0:
                column = jnp.broadcast_to(rows[:, at : at + 1], (BASE, 128))
                following = jnp.broadcast_to(rows[:, at + 1 : at + 2], (BASE, 128))
            recip = 1.0 / column[step : step + 1, :]
            if step + 2 < BASE:
                ahead = jnp.broadcast_to(rows[:, at + 2 : at + 3], (BASE, 128))
            scaled = jnp.where(here, 1.0, pivot_row) * jnp.concatenate([recip, recip], axis=1)
            both = jnp.concatenate([column, column], axis=1)
            rows = jnp.where(sub == step, scaled, jnp.where(here, 0.0, rows) - both * scaled)

            def turn(value):
                turned = value[step : step + 1, :] * recip
                return jnp.where(sub == step, turned, value - column * turned)

            if step + 1 < BASE:
                turned_next = turn(following)
                if step + 2 < BASE:
                    following = turn(ahead)
                column = turned_next
        in_block = (lanes >= base) & (lanes < base + BASE)
        full = inv_ref[...]
        left = jnp.where(in_block, full, 0.0)
        kept = jnp.where(in_block, 0.0, full)
        parts = []
        if base:
            parts.append(jnp.zeros((base, PIVOTS), F32))
        parts.append(rows)
        if base + BASE < PIVOTS:
            parts.append(jnp.zeros((PIVOTS - base - BASE, PIVOTS), F32))
        inv_ref[...] = kept - exact(left, jnp.concatenate(parts, axis=0))
        inv_ref[base : base + BASE, :] = rows
    relative = (iota((PIVOTS, slots), 0) == slot_rel_ref[...]).astype(F32)
    inv_rel_ref[...] = exact(inv_ref[...], relative)


def invert(slot_abs, slot_rel, piv):
    slots = piv.shape[0]
    return pl.pallas_call(
        inverse_kernel,
        out_shape=(
            jax.ShapeDtypeStruct((PIVOTS, PIVOTS), F32),
            jax.ShapeDtypeStruct((PIVOTS, slots), F32),
        ),
        compiler_params=BIG,
    )(slot_abs, slot_rel, piv)


OFFSETS = (0, 3, 1, 2)


def lower_kernel(active_ref, inv_ref, inv_rel_ref, current_ref, first_ref, lower_ref):
    active = active_ref[...] > 0
    current = current_ref[...]
    first_ref[...] = jnp.where(active, dot3(current, inv_ref[...]), current)
    high, low = halves(jnp.where(active, dot3(current, inv_rel_ref[...]), 0.0))
    slots = high.shape[1]
    lower_ref[:, :slots] = high
    lower_ref[:, slots : 2 * slots] = high
    lower_ref[:, 2 * slots :] = low


def lower_factor(active, inv, inv_rel, front_rows):
    rows = front_rows.shape[0]
    slots = inv_rel.shape[1]
    whole = lambda shape: pl.BlockSpec(shape, lambda i: (0, 0))
    return pl.pallas_call(
        lower_kernel,
        grid=(1,),
        in_specs=[whole(active.shape), whole(inv.shape), whole(inv_rel.shape), whole((rows, PIVOTS))],
        out_specs=[whole((rows, PIVOTS)), whole((rows, 3 * slots))],
        out_shape=(
            jax.ShapeDtypeStruct((rows, PIVOTS), F32),
            jax.ShapeDtypeStruct((rows, 3 * slots), BF16),
        ),
        compiler_params=BIG,
    )(active, inv, inv_rel, front_rows)


def eliminate_kernel(
    place_ref, first_ref, lower_ref, rank_hbm, front_hbm, *refs
):
    pieces, refs = refs[:10], refs[10:]
    factors_hbm, send_hbm = refs[:2]
    matrix, upper, ranks, sorted_in, moves, send = refs[2:8]
    front_sem, upper_sem, rank_sem, factors_sem, send_sem = refs[8:]
    rows, width = matrix.shape
    half = width // 2
    slots = upper.shape[0]
    tile = 256
    tiles = width // tile

    loads = []
    for part in range(2):
        at = part * half
        loads.append(
            pltpu.make_async_copy(
                front_hbm.at[:, PIVOTS + at : PIVOTS + at + half], matrix.at[:, at : at + half], front_sem.at[part]
            )
        )
    rank_load = pltpu.make_async_copy(rank_hbm, ranks, rank_sem)
    upper_loads = []
    for part in range(2):
        into = slice(part * half, (part + 1) * half)
        for piece in range(4):
            for block in range(4):
                if piece < 3:
                    source, at = pieces[part * 5 + piece], block * CAP
                else:
                    source, at = pieces[part * 5 + 3 + block // 2], block % 2 * CAP
                slot = ((block * 4 + piece) if part == 0 else (piece * 4 + block)) * CAP
                upper_loads.append(
                    pltpu.make_async_copy(
                        source.at[at : at + CAP, :], upper.at[slot : slot + CAP, into], upper_sem.at[part * 16 + piece * 4 + block]
                    )
                )
    for part in range(2):
        for load in upper_loads[part * 16 : part * 16 + 16]:
            load.start()
        loads[part].start()
        if part == 0:
            rank_load.start()
    stores = [pltpu.make_async_copy(first_ref, factors_hbm.at[:, :PIVOTS], factors_sem.at[0])]
    stores[0].start()
    place = (iota((rows, rows), 0) == place_ref[...]).astype(F32).astype(BF16)
    lower_high, lower_low = lower_ref[:, : 2 * slots], lower_ref[:, 2 * slots :]

    def update(at, size):
        high, low = halves(upper[:, at : at + size])
        change = dot16(lower_high, jnp.concatenate([high, low], axis=0)) + dot16(lower_low, high)
        out = matrix[:, at : at + size] - change
        matrix[:, at : at + size] = out
        high, low = halves(out)
        placed = dot16(place, jnp.concatenate([high, low], axis=1)).astype(BF16)
        sorted_in[:rows, at : at + size] = placed[:, :size]
        sorted_in[rows:, at : at + size] = placed[:, size:]

    def generate(slot, index):
        lane = iota((1, 128), 1) + index * tile
        for part in range(2):
            moves[slot, :, part * 128 : (part + 1) * 128] = (
                (ranks[...] == lane + part * 128).astype(F32).astype(BF16)
            )

    def ready(part):
        loads[part].wait()
        for load in upper_loads[part * 16 : part * 16 + 16]:
            load.wait()

    def store(part):
        at = part * half
        stores.append(
            pltpu.make_async_copy(
                matrix.at[:, at : at + half],
                factors_hbm.at[:, PIVOTS + at : PIVOTS + at + half],
                factors_sem.at[part + 1],
            )
        )
        stores[-1].start()

    span = 768
    ready(0)
    for at in range(0, width, span):
        if at < half < at + span:
            rank_load.wait()
            generate(0, 0)
            ready(1)
        update(at, span)
        if at < half <= at + span:
            store(0)
    store(1)

    def permute(slot, index):
        at = pl.multiple_of(index * tile, tile)
        out = dot16(sorted_in[...], moves[slot])
        send[:, :, pl.ds(at, tile)] = (out[:rows] + out[rows:]).reshape(rows // 2, 2, tile)
        pltpu.make_async_copy(
            send.at[:, :, pl.ds(at, tile)], send_hbm.at[:, :, pl.ds(at, tile)], send_sem.at[index]
        ).start()

    def pair(index, carry):
        generate(1, 2 * index + 1)
        permute(0, 2 * index)
        generate(0, 2 * index + 2)
        permute(1, 2 * index + 1)
        return carry

    lax.fori_loop(0, tiles // 2, pair, 0)
    permute(0, tiles - 1)
    for store in stores:
        store.wait()
    for index in range(tiles):
        at = index * tile
        pltpu.make_async_copy(
            send.at[:, :, at : at + tile], send_hbm.at[:, :, at : at + tile], send_sem.at[index]
        ).wait()


def eliminate(place, rank, first, lower, front_rows, line, file):
    rows, columns = front_rows.shape
    width = columns - PIVOTS
    vmem = pl.BlockSpec(memory_space=pltpu.VMEM)
    hbm = pl.BlockSpec(memory_space=pl.ANY)
    return pl.pallas_call(
        eliminate_kernel,
        in_specs=[vmem] * 3 + [hbm] * 12,
        out_specs=(hbm, hbm),
        out_shape=(
            jax.ShapeDtypeStruct((rows, columns), F32),
            jax.ShapeDtypeStruct((rows // 2, 2, width), F32),
        ),
        scratch_shapes=[
            pltpu.VMEM((rows, width), F32),
            pltpu.VMEM((16 * CAP, width), F32),
            pltpu.VMEM(rank.shape, I32),
            pltpu.VMEM((2 * rows, width), BF16),
            pltpu.VMEM((2, width, 256), BF16),
            pltpu.VMEM((rows // 2, 2, width), F32),
            pltpu.SemaphoreType.DMA((2,)),
            pltpu.SemaphoreType.DMA((32,)),
            pltpu.SemaphoreType.DMA,
            pltpu.SemaphoreType.DMA((3,)),
            pltpu.SemaphoreType.DMA((width // 256,)),
        ],
        compiler_params=BIG,
    )(place, first, lower, rank, front_rows, *line, *file)


def assemble_kernel(group_ref, source_ref, put_ref, received_ref, parent_ref, out_ref):
    fronts = source_ref.shape[0]
    senders = received_ref.shape[0] // fronts
    per_front = senders * received_ref.shape[1]
    last = received_ref.shape[2] // 128 - 1
    first = pl.program_id(0) * (out_ref.shape[1] // 128)
    put = put_ref[...]
    for tile in range(out_ref.shape[1] // 256):
        columns = []
        for part in (2 * tile, 2 * tile + 1):
            pieces = []
            for front in range(fronts):
                group = jnp.minimum(group_ref[front, first + part], last)
                following = jnp.minimum(group + 1, last)
                source = source_ref[front : front + 1, part * 128 : (part + 1) * 128]
                lane = jnp.broadcast_to(source & 127, (per_front, 128))
                which = source >> 7
                span = slice(front * senders, (front + 1) * senders)
                near = received_ref[span, :, pl.ds(pl.multiple_of(group * 128, 128), 128)].reshape(per_front, 128)
                far = received_ref[span, :, pl.ds(pl.multiple_of(following * 128, 128), 128)].reshape(per_front, 128)
                near = jnp.take_along_axis(near, lane, axis=1)
                far = jnp.take_along_axis(far, lane, axis=1)
                pieces.append(jnp.where(which == group, near, jnp.where(which == following, far, 0.0)))
            columns.append(jnp.concatenate(pieces, axis=0))
        high, low = halves(jnp.concatenate(columns, axis=1))
        at = slice(tile * 256, (tile + 1) * 256)
        out_ref[:, at] = parent_ref[:, at] + (dot16(put, high) + dot16(put, low))


def assemble(group, source, put, received, parent):
    rows, width = parent.shape
    fronts = source.shape[0]
    tile = 2048
    return pl.pallas_call(
        assemble_kernel,
        grid_spec=pltpu.PrefetchScalarGridSpec(
            num_scalar_prefetch=1,
            grid=(width // tile,),
            in_specs=[
                pl.BlockSpec((fronts, tile), lambda i, g: (0, i)),
                pl.BlockSpec(put.shape, lambda i, g: (0, 0)),
                pl.BlockSpec(received.shape, lambda i, g: (0, 0, 0)),
                pl.BlockSpec((rows, tile), lambda i, g: (0, i)),
            ],
            out_specs=pl.BlockSpec((rows, tile), lambda i, g: (0, i)),
        ),
        out_shape=jax.ShapeDtypeStruct((rows, width), F32),
        compiler_params=BIG,
    )(group, source, put, received, parent)


def columns_below(child_map, parent_width):
    high_iota = jnp.arange(parent_width // 128, dtype=I32)
    low_iota = jnp.arange(128, dtype=I32)
    in_high = ((child_map >> 7)[:, :, None] == high_iota).astype(BF16)
    in_low = ((child_map & 127)[:, :, None] == low_iota).astype(BF16)
    counts = jnp.einsum("fah,fal->fhl", in_high, in_low, preferred_element_type=F32)
    within = jnp.einsum(
        "fhl,lm->fhm",
        counts.astype(BF16),
        (low_iota[:, None] < low_iota[None, :]).astype(BF16),
        preferred_element_type=F32,
    )
    starts = jnp.einsum(
        "fh,hg->fg",
        jnp.sum(counts, axis=2).astype(BF16),
        (high_iota[:, None] < high_iota[None, :]).astype(BF16),
        preferred_element_type=F32,
    )
    return starts[:, :, None] + within, counts


def local(front, row_list, child_map, parent):
    front_rows = front[0]
    rows = front_rows.shape[0]
    width = front_rows.shape[1] - PIVOTS
    helpers = lax.axis_size("helper")
    fronts = lax.axis_size("front")
    devices = helpers * fronts
    cap = (rows + devices - 1) // devices
    parent_rows, parent_width = parent.shape
    my_front = lax.axis_index("front")
    my_helper = lax.axis_index("helper")
    me = my_front * helpers + my_helper
    order = jnp.take(row_list, my_front, axis=0)
    by_helper = order.reshape(helpers, rows)
    own_ids = lax.dynamic_slice_in_dim(order, my_helper * rows, rows)

    pivot, first, second = select_panel(own_ids, front_rows)
    own_map = jnp.take(child_map, my_front, axis=0)
    piv = lax.all_to_all(pivot, "helper", split_axis=0, concat_axis=0, tiled=True)
    piv = piv.reshape(helpers * CAP, PIVOTS)
    firsts = (first, shift(first, X_UP), shift(first, X_DOWN), shift(first, X_FAR))
    seconds = (second, shift(second, Y_UP), shift(second, Y_DOWN), shift(second, Y_FAR))

    inside = by_helper < PIVOTS
    earlier = (jnp.arange(rows)[:, None] < jnp.arange(rows)[None, :]).astype(BF16)
    slot_rank = dot16(inside.astype(BF16), earlier).astype(I32)
    slot_iota = jnp.arange(CAP, dtype=I32)
    hit = (slot_rank[:, None, :] == slot_iota[None, :, None]) & inside[:, None, :]
    slot_row = jnp.sum(jnp.where(hit, by_helper[:, None, :] + 1, 0), axis=2) - 1
    grid_iota = jnp.array(OFFSETS, I32)
    source_x = (my_helper // GRID + grid_iota) % GRID
    source_y = (my_helper % GRID + grid_iota) % GRID
    relative = (source_x[:, None] * GRID + source_y[None, :]).reshape(helpers)
    slot_rel = jnp.sum(
        jnp.where((relative[:, None] == jnp.arange(helpers)[None, :])[:, :, None], slot_row[None], 0), axis=1
    )
    rank = column_ranks(own_map)
    slot_row, slot_rel = slot_row.reshape(1, -1), slot_rel.reshape(1, -1)
    firsts, seconds, rank, slot_row, slot_rel, piv = lax.optimization_barrier(
        (firsts, seconds, rank, slot_row, slot_rel, piv)
    )

    line, file = pack(firsts, seconds)
    line_up, line_down = shift(line, Y_UP), shift(line, Y_DOWN)
    file_up, file_down = shift(file, X_UP), shift(file, X_DOWN)
    inv, inv_rel = invert(slot_row, slot_rel, piv)
    line_up, line_down, file_up, file_down, inv, inv_rel = lax.optimization_barrier(
        (line_up, line_down, file_up, file_down, inv, inv_rel)
    )
    up, down, left, right = cut(line_up, line_down, file_up, file_down)
    line = (line, line_up, line_down, shift(up, Y_UP), shift(down, Y_DOWN))
    file = (file, file_up, file_down, shift(left, X_UP), shift(right, X_DOWN))

    own_cb = own_ids >= PIVOTS
    column_iota = jnp.arange(width, dtype=I32)
    own_target = jnp.sum(
        jnp.where((own_ids - PIVOTS)[:, None] == column_iota[None, :], own_map[None, :], 0), axis=1
    )
    owner = jnp.where(own_cb, own_target // parent_rows, -1)
    row_iota = jnp.arange(rows, dtype=I32)
    same = (owner[:, None] == owner[None, :]) & (row_iota[None, :] < row_iota[:, None])
    place = jnp.where(own_cb, owner * cap + jnp.sum(same.astype(I32), axis=1), -1)

    first_columns, lower = lower_factor(own_cb[:, None].astype(I32), inv, inv_rel, front_rows)
    factors, outgoing = eliminate(place[None, :], rank, first_columns, lower, front_rows, line, file)
    received = lax.all_to_all(outgoing, ("front", "helper"), split_axis=0, concat_axis=0, tiled=True)

    below, counts = columns_below(child_map, parent_width)
    source = jnp.where(counts > 0, below, -1.0).astype(I32).reshape(fronts, parent_width)
    group = below[:, :, 0].astype(I32) >> 7

    own_parent = me * parent_rows + jnp.arange(parent_rows, dtype=I32)
    column = jnp.sum(
        jnp.where(child_map[:, None, :] == own_parent[None, :, None], column_iota + 1, 0), axis=2
    )
    found = column > 0
    stored = jnp.sum(
        jnp.where(
            row_list[:, None, :] == (column + (PIVOTS - 1))[:, :, None],
            jnp.arange(row_list.shape[1], dtype=I32),
            0,
        ),
        axis=2,
    )
    sender = stored // rows
    ahead = jnp.sum(
        (
            found[:, None, :]
            & (sender[:, :, None] == sender[:, None, :])
            & (stored[:, None, :] < stored[:, :, None])
        ).astype(I32),
        axis=2,
    )
    front_iota = jnp.arange(fronts, dtype=I32)
    slot = jnp.where(found, (front_iota[:, None] * helpers + sender) * cap + ahead, -1)
    put = jnp.any(slot[:, :, None] == jnp.arange(devices * cap, dtype=I32), axis=0).astype(BF16)
    assembled = assemble(group, source, put, received, parent)
    return (factors[None], assembled)


def solution(mesh):
    in_specs = (P("front", "helper", None), P(), P(), P(("front", "helper"), None))
    out_specs = (P("front", "helper", None), P(("front", "helper"), None))
    return jax.shard_map(local, mesh=mesh, in_specs=in_specs, out_specs=out_specs, check_vma=False)
```

```python
import jax
import jax.numpy as jnp
from jax import lax
from jax.experimental import pallas as pl
from jax.experimental.pallas import tpu as pltpu
from jax.sharding import PartitionSpec as P

PIVOTS = 256
CAP = 24
BASE = 32
F32 = jnp.float32
BF16 = jnp.bfloat16
I32 = jnp.int32
GRID = 4
X_UP, X_DOWN, X_FAR = (1, 0), (3, 0), (2, 0)
Y_UP, Y_DOWN, Y_FAR = (0, 1), (0, 3), (0, 2)
BIG = pltpu.CompilerParams(vmem_limit_bytes=58 << 20)


def iota(shape, axis):
    return lax.broadcasted_iota(I32, shape, axis)


def exact(left, right):
    return jnp.dot(left, right, precision=lax.Precision.HIGHEST, preferred_element_type=F32)


def halves(value):
    high = value.astype(BF16)
    return high, (value - high.astype(F32)).astype(BF16)


def dot16(left, right):
    return jnp.dot(left, right, preferred_element_type=F32)


def dot3(left, right):
    left_high, left_low = halves(left)
    right_high, right_low = halves(right)
    return dot16(left_high, right_high) + (dot16(left_high, right_low) + dot16(left_low, right_high))


def select_kernel(ids_ref, front_ref, pivot_ref, first_ref, second_ref):
    rows = front_ref.shape[0]
    ids = ids_ref[...]
    inside = jnp.broadcast_to((ids < PIVOTS).astype(F32), (8, rows)).astype(BF16)
    before = (iota((rows, rows), 0) < iota((rows, rows), 1)).astype(F32).astype(BF16)
    rank = dot16(inside, before)[:1].astype(I32)
    rank = jnp.where(ids < PIVOTS, rank, -1)
    chosen = (jnp.broadcast_to(rank, (CAP, rows)) == iota((CAP, rows), 0)).astype(F32).astype(BF16)

    def pick(start, into):
        step = 512
        for at in range(0, into.shape[1], step):
            stop = min(at + step, into.shape[1])
            value = front_ref[:, start + at : start + stop]
            high = value.astype(BF16)
            middle, low = halves(value - high.astype(F32))
            into[:, at:stop] = dot16(chosen, high) + (dot16(chosen, middle) + dot16(chosen, low))

    high = front_ref[:, :PIVOTS].astype(BF16)
    middle, low = halves(front_ref[:, :PIVOTS] - high.astype(F32))
    pivot = dot16(chosen, high) + (dot16(chosen, middle) + dot16(chosen, low))
    for helper in range(pivot_ref.shape[0]):
        pivot_ref[helper] = pivot
    pick(PIVOTS, first_ref)
    pick(PIVOTS + first_ref.shape[1], second_ref)


def select_panel(own_ids, front_rows):
    half = (front_rows.shape[1] - PIVOTS) // 2
    return pl.pallas_call(
        select_kernel,
        out_shape=(
            jax.ShapeDtypeStruct((GRID * GRID, CAP, PIVOTS), F32),
            jax.ShapeDtypeStruct((CAP, half), F32),
            jax.ShapeDtypeStruct((CAP, half), F32),
        ),
        compiler_params=BIG,
    )(own_ids[None, :], front_rows)


def shift_pairs(step):
    return [
        (x * GRID + y, (x + step[0]) % GRID * GRID + (y + step[1]) % GRID)
        for x in range(GRID)
        for y in range(GRID)
    ]


def shift(value, step):
    return lax.ppermute(value, "helper", shift_pairs(step))


def pack_kernel(*refs):
    for index in range(8):
        into = slice(index % 4 * CAP, (index % 4 + 1) * CAP)
        refs[8 + index // 4][into, :] = refs[index][...]


def pack(firsts, seconds):
    half = seconds[0].shape[1]
    return pl.pallas_call(
        pack_kernel,
        out_shape=(jax.ShapeDtypeStruct((4 * CAP, half), F32),) * 2,
        compiler_params=BIG,
    )(*firsts, *seconds)


def rank_kernel(map_ref, rank_ref):
    width = map_ref.shape[1]
    high = (iota((64, width), 0) == (map_ref[...] >> 7)).astype(F32).astype(BF16)
    in_low = iota((128, width), 0) == (map_ref[...] & 127)
    low = in_low.astype(F32).astype(BF16)
    counts = lax.dot_general(high, low, (((1,), (1,)), ((), ())), preferred_element_type=F32)
    before = (iota((128, 128), 0) < iota((128, 128), 1)).astype(F32).astype(BF16)
    within = dot16(counts.astype(BF16), before)
    earlier = (iota((64, 64), 1) < iota((64, 64), 0)).astype(F32).astype(BF16)
    starts = jnp.sum(dot16(earlier, counts.astype(BF16)), axis=1, keepdims=True)
    below = (starts + within).astype(I32)
    coarse = (below >> 6).astype(F32).astype(BF16)
    fine = (below & 63).astype(F32).astype(BF16)
    contract = (((0,), (0,)), ((), ()))
    table = 64.0 * lax.dot_general(coarse, high, contract, preferred_element_type=F32)
    table = table + lax.dot_general(fine, high, contract, preferred_element_type=F32)
    row = jnp.sum(jnp.where(in_low, table, 0.0), axis=0, keepdims=True)
    for start in range(0, width, 128):
        block = jnp.broadcast_to(row[:, start : start + 128], (128, 128))
        rank_ref[start : start + 128, :] = block.T.astype(I32)


def column_ranks(own_map):
    width = own_map.shape[0]
    return pl.pallas_call(
        rank_kernel, out_shape=jax.ShapeDtypeStruct((width, 128), I32), compiler_params=BIG
    )(own_map[None, :])


def pivot_steps(inv_ref, blocks):
    lanes = iota((1, PIVOTS), 1)
    for block in blocks:
        base = block * BASE
        rows = inv_ref[base : base + BASE, :]
        sub = iota((BASE, 1), 0)
        for step in range(BASE):
            at = base + step
            here = lanes == at
            pivot_row = rows[step : step + 1, :]
            if step == 0:
                column = jnp.broadcast_to(rows[:, at : at + 1], (BASE, 128))
                following = jnp.broadcast_to(rows[:, at + 1 : at + 2], (BASE, 128))
            recip = 1.0 / column[step : step + 1, :]
            if step + 2 < BASE:
                ahead = jnp.broadcast_to(rows[:, at + 2 : at + 3], (BASE, 128))
            scaled = jnp.where(here, 1.0, pivot_row) * jnp.concatenate([recip, recip], axis=1)
            both = jnp.concatenate([column, column], axis=1)
            rows = jnp.where(sub == step, scaled, jnp.where(here, 0.0, rows) - both * scaled)

            def turn(value):
                turned = value[step : step + 1, :] * recip
                return jnp.where(sub == step, turned, value - column * turned)

            if step + 1 < BASE:
                turned_next = turn(following)
                if step + 2 < BASE:
                    following = turn(ahead)
                column = turned_next
        in_block = (lanes >= base) & (lanes < base + BASE)
        full = inv_ref[...]
        left = jnp.where(in_block, full, 0.0)
        kept = jnp.where(in_block, 0.0, full)
        parts = []
        if base:
            parts.append(jnp.zeros((base, PIVOTS), F32))
        parts.append(rows)
        if base + BASE < PIVOTS:
            parts.append(jnp.zeros((PIVOTS - base - BASE, PIVOTS), F32))
        inv_ref[...] = kept - exact(left, jnp.concatenate(parts, axis=0))
        inv_ref[base : base + BASE, :] = rows


def first_steps_kernel(slot_ref, piv_ref, inv_ref):
    natural = (iota((PIVOTS, piv_ref.shape[0]), 0) == slot_ref[...]).astype(F32)
    inv_ref[...] = exact(natural, piv_ref[...])
    pivot_steps(inv_ref, range(PIVOTS // BASE // 2))


def first_steps(slot_abs, piv):
    return pl.pallas_call(
        first_steps_kernel, out_shape=jax.ShapeDtypeStruct((PIVOTS, PIVOTS), F32), compiler_params=BIG
    )(slot_abs, piv)


def last_steps_kernel(slot_ref, half_ref, inv_ref, inv_rel_ref):
    inv_ref[...] = half_ref[...]
    pivot_steps(inv_ref, range(PIVOTS // BASE // 2, PIVOTS // BASE))
    relative = (iota(inv_rel_ref.shape, 0) == slot_ref[...]).astype(F32)
    inv_rel_ref[...] = exact(inv_ref[...], relative)


def last_steps(slot_rel, half):
    return pl.pallas_call(
        last_steps_kernel,
        out_shape=(
            jax.ShapeDtypeStruct((PIVOTS, PIVOTS), F32),
            jax.ShapeDtypeStruct((PIVOTS, slot_rel.shape[1]), F32),
        ),
        compiler_params=BIG,
    )(slot_rel, half)


OFFSETS = (0, 3, 1, 2)


def lower_kernel(active_ref, inv_ref, inv_rel_ref, current_ref, first_ref, lower_ref):
    active = active_ref[...] > 0
    current = current_ref[...]
    first_ref[...] = jnp.where(active, dot3(current, inv_ref[...]), current)
    high, low = halves(jnp.where(active, dot3(current, inv_rel_ref[...]), 0.0))
    slots = high.shape[1]
    lower_ref[:, :slots] = high
    lower_ref[:, slots : 2 * slots] = high
    lower_ref[:, 2 * slots :] = low


def lower_factor(active, inv, inv_rel, front_rows):
    rows = front_rows.shape[0]
    slots = inv_rel.shape[1]
    whole = lambda shape: pl.BlockSpec(shape, lambda i: (0, 0))
    return pl.pallas_call(
        lower_kernel,
        grid=(1,),
        in_specs=[whole(active.shape), whole(inv.shape), whole(inv_rel.shape), whole((rows, PIVOTS))],
        out_specs=[whole((rows, PIVOTS)), whole((rows, 3 * slots))],
        out_shape=(
            jax.ShapeDtypeStruct((rows, PIVOTS), F32),
            jax.ShapeDtypeStruct((rows, 3 * slots), BF16),
        ),
        compiler_params=BIG,
    )(active, inv, inv_rel, front_rows)


def eliminate_kernel(
    place_ref, first_ref, lower_ref, rank_hbm, front_hbm, *refs
):
    pieces, refs = refs[:8], refs[8:]
    factors_hbm, send_hbm = refs[:2]
    matrix, upper, ranks, sorted_in, moves, send = refs[2:8]
    front_sem, upper_sem, rank_sem, factors_sem, send_sem = refs[8:]
    rows, width = matrix.shape
    half = width // 2
    slots = upper.shape[0]
    tile = moves.shape[2]
    tiles = width // tile

    loads = []
    for part in range(2):
        at = part * half
        loads.append(
            pltpu.make_async_copy(
                front_hbm.at[:, PIVOTS + at : PIVOTS + at + half], matrix.at[:, at : at + half], front_sem.at[part]
            )
        )
    rank_load = pltpu.make_async_copy(rank_hbm, ranks, rank_sem)
    upper_loads = []
    for part in range(2):
        into = slice(part * half, (part + 1) * half)
        for piece in range(4):
            for block in range(4):
                source, at = pieces[part * 4 + piece], block * CAP
                slot = ((block * 4 + piece) if part == 0 else (piece * 4 + block)) * CAP
                upper_loads.append(
                    pltpu.make_async_copy(
                        source.at[at : at + CAP, :], upper.at[slot : slot + CAP, into], upper_sem.at[part * 16 + piece * 4 + block]
                    )
                )
    for part in range(2):
        for load in upper_loads[part * 16 : part * 16 + 16]:
            load.start()
        loads[part].start()
        if part == 0:
            rank_load.start()
    stores = [pltpu.make_async_copy(first_ref, factors_hbm.at[:, :PIVOTS], factors_sem.at[0])]
    stores[0].start()
    place = (iota((rows, rows), 0) == place_ref[...]).astype(F32).astype(BF16)
    lower_high, lower_low = lower_ref[:, : 2 * slots], lower_ref[:, 2 * slots :]

    def update(at, size):
        high, low = halves(upper[:, at : at + size])
        change = dot16(lower_high, jnp.concatenate([high, low], axis=0)) + dot16(lower_low, high)
        out = matrix[:, at : at + size] - change
        matrix[:, at : at + size] = out
        high, low = halves(out)
        placed = dot16(place, jnp.concatenate([high, low], axis=1)).astype(BF16)
        sorted_in[:rows, at : at + size] = placed[:, :size]
        sorted_in[rows:, at : at + size] = placed[:, size:]

    def generate(slot, index):
        lane = iota((1, 128), 1) + index * tile
        for part in range(tile // 128):
            moves[slot, :, part * 128 : (part + 1) * 128] = (
                (ranks[...] == lane + part * 128).astype(F32).astype(BF16)
            )

    def ready(part):
        loads[part].wait()
        for load in upper_loads[part * 16 : part * 16 + 16]:
            load.wait()

    def store(part):
        at = part * half
        stores.append(
            pltpu.make_async_copy(
                matrix.at[:, at : at + half],
                factors_hbm.at[:, PIVOTS + at : PIVOTS + at + half],
                factors_sem.at[part + 1],
            )
        )
        stores[-1].start()

    span = 768
    ready(0)
    for at in range(0, width, span):
        if at < half < at + span:
            rank_load.wait()
            generate(0, 0)
            ready(1)
        update(at, span)
        if at < half <= at + span:
            store(0)
    store(1)

    def permute(slot, index):
        at = pl.multiple_of(index * tile, tile)
        out = dot16(sorted_in[...], moves[slot])
        send[:, :, pl.ds(at, tile)] = (out[:rows] + out[rows:]).reshape(rows // 2, 2, tile)
        pltpu.make_async_copy(
            send.at[:, :, pl.ds(at, tile)], send_hbm.at[:, :, pl.ds(at, tile)], send_sem.at[index]
        ).start()

    def pair(index, carry):
        generate(1, 2 * index + 1)
        permute(0, 2 * index)
        generate(0, 2 * index + 2)
        permute(1, 2 * index + 1)
        return carry

    lax.fori_loop(0, tiles // 2, pair, 0)
    permute(0, tiles - 1)
    for store in stores:
        store.wait()
    for index in range(tiles):
        at = index * tile
        pltpu.make_async_copy(
            send.at[:, :, at : at + tile], send_hbm.at[:, :, at : at + tile], send_sem.at[index]
        ).wait()


def eliminate(place, rank, first, lower, front_rows, line, file):
    rows, columns = front_rows.shape
    width = columns - PIVOTS
    vmem = pl.BlockSpec(memory_space=pltpu.VMEM)
    hbm = pl.BlockSpec(memory_space=pl.ANY)
    return pl.pallas_call(
        eliminate_kernel,
        in_specs=[vmem] * 3 + [hbm] * 10,
        out_specs=(hbm, hbm),
        out_shape=(
            jax.ShapeDtypeStruct((rows, columns), F32),
            jax.ShapeDtypeStruct((rows // 2, 2, width), F32),
        ),
        scratch_shapes=[
            pltpu.VMEM((rows, width), F32),
            pltpu.VMEM((16 * CAP, width), F32),
            pltpu.VMEM(rank.shape, I32),
            pltpu.VMEM((2 * rows, width), BF16),
            pltpu.VMEM((2, width, 768), BF16),
            pltpu.VMEM((rows // 2, 2, width), F32),
            pltpu.SemaphoreType.DMA((2,)),
            pltpu.SemaphoreType.DMA((32,)),
            pltpu.SemaphoreType.DMA,
            pltpu.SemaphoreType.DMA((3,)),
            pltpu.SemaphoreType.DMA((width // 256,)),
        ],
        compiler_params=BIG,
    )(place, first, lower, rank, front_rows, *line, *file)


def assemble_kernel(start_ref, source_ref, put_ref, received_ref, parent_ref, out_ref):
    fronts = source_ref.shape[0]
    senders = received_ref.shape[0] // fronts
    per_front = senders * received_ref.shape[1]
    last = received_ref.shape[2] // 128 - 1
    first = pl.program_id(0) * (out_ref.shape[1] // 128)
    put = put_ref[...]
    for tile in range(out_ref.shape[1] // 256):
        columns = []
        for part in (2 * tile, 2 * tile + 1):
            pieces = []
            for front in range(fronts):
                base = start_ref[front, first + part]
                group = jnp.minimum(base >> 7, last)
                following = jnp.minimum(group + 1, last)
                source = source_ref[front : front + 1, part * 128 : (part + 1) * 128]
                lane = jnp.broadcast_to(source & 127, (per_front, 128))
                span = slice(front * senders, (front + 1) * senders)
                near = received_ref[span, :, pl.ds(pl.multiple_of(group * 128, 128), 128)]
                far = received_ref[span, :, pl.ds(pl.multiple_of(following * 128, 128), 128)]
                window = jnp.where(iota((1, 1, 128), 2) >= (base & 127), near, far).reshape(per_front, 128)
                value = jnp.take_along_axis(window, lane, axis=1)
                pieces.append(jnp.where(source >= 0, value, 0.0))
            columns.append(jnp.concatenate(pieces, axis=0))
        high, low = halves(jnp.concatenate(columns, axis=1))
        at = slice(tile * 256, (tile + 1) * 256)
        out_ref[:, at] = parent_ref[:, at] + (dot16(put, high) + dot16(put, low))


def assemble(start, source, put, received, parent):
    rows, width = parent.shape
    fronts = source.shape[0]
    tile = 2048
    return pl.pallas_call(
        assemble_kernel,
        grid_spec=pltpu.PrefetchScalarGridSpec(
            num_scalar_prefetch=1,
            grid=(width // tile,),
            in_specs=[
                pl.BlockSpec((fronts, tile), lambda i, g: (0, i)),
                pl.BlockSpec(put.shape, lambda i, g: (0, 0)),
                pl.BlockSpec(received.shape, lambda i, g: (0, 0, 0)),
                pl.BlockSpec((rows, tile), lambda i, g: (0, i)),
            ],
            out_specs=pl.BlockSpec((rows, tile), lambda i, g: (0, i)),
        ),
        out_shape=jax.ShapeDtypeStruct((rows, width), F32),
        compiler_params=BIG,
    )(start, source, put, received, parent)


def columns_below(child_map, parent_width):
    high_iota = jnp.arange(parent_width // 128, dtype=I32)
    low_iota = jnp.arange(128, dtype=I32)
    in_high = ((child_map >> 7)[:, :, None] == high_iota).astype(BF16)
    in_low = ((child_map & 127)[:, :, None] == low_iota).astype(BF16)
    counts = jnp.einsum("fah,fal->fhl", in_high, in_low, preferred_element_type=F32)
    within = jnp.einsum(
        "fhl,lm->fhm",
        counts.astype(BF16),
        (low_iota[:, None] < low_iota[None, :]).astype(BF16),
        preferred_element_type=F32,
    )
    starts = jnp.einsum(
        "fh,hg->fg",
        jnp.sum(counts, axis=2).astype(BF16),
        (high_iota[:, None] < high_iota[None, :]).astype(BF16),
        preferred_element_type=F32,
    )
    return starts[:, :, None] + within, counts


def local(front, row_list, child_map, parent):
    front_rows = front[0]
    rows = front_rows.shape[0]
    width = front_rows.shape[1] - PIVOTS
    helpers = lax.axis_size("helper")
    fronts = lax.axis_size("front")
    devices = helpers * fronts
    cap = (rows + devices - 1) // devices
    parent_rows, parent_width = parent.shape
    my_front = lax.axis_index("front")
    my_helper = lax.axis_index("helper")
    me = my_front * helpers + my_helper
    order = jnp.take(row_list, my_front, axis=0)
    by_helper = order.reshape(helpers, rows)
    own_ids = lax.dynamic_slice_in_dim(order, my_helper * rows, rows)

    pivot, first, second = select_panel(own_ids, front_rows)
    own_map = jnp.take(child_map, my_front, axis=0)
    piv = lax.all_to_all(pivot, "helper", split_axis=0, concat_axis=0, tiled=True)
    piv = piv.reshape(helpers * CAP, PIVOTS)
    firsts = (first, shift(first, X_UP), shift(first, X_DOWN), shift(first, X_FAR))
    seconds = (second, shift(second, Y_UP), shift(second, Y_DOWN), shift(second, Y_FAR))

    inside = by_helper < PIVOTS
    earlier = (jnp.arange(rows)[:, None] < jnp.arange(rows)[None, :]).astype(BF16)
    slot_rank = dot16(inside.astype(BF16), earlier).astype(I32)
    slot_iota = jnp.arange(CAP, dtype=I32)
    hit = (slot_rank[:, None, :] == slot_iota[None, :, None]) & inside[:, None, :]
    slot_row = jnp.sum(jnp.where(hit, by_helper[:, None, :] + 1, 0), axis=2) - 1
    grid_iota = jnp.array(OFFSETS, I32)
    source_x = (my_helper // GRID + grid_iota) % GRID
    source_y = (my_helper % GRID + grid_iota) % GRID
    relative = (source_x[:, None] * GRID + source_y[None, :]).reshape(helpers)
    slot_rel = jnp.sum(
        jnp.where((relative[:, None] == jnp.arange(helpers)[None, :])[:, :, None], slot_row[None], 0), axis=1
    )
    rank = column_ranks(own_map)
    slot_row, slot_rel = slot_row.reshape(1, -1), slot_rel.reshape(1, -1)
    firsts, seconds, rank, slot_row, slot_rel, piv = lax.optimization_barrier(
        (firsts, seconds, rank, slot_row, slot_rel, piv)
    )

    line, file = pack(firsts, seconds)
    line_up, line_down = shift(line, Y_UP), shift(line, Y_DOWN)
    file_up, file_down = shift(file, X_UP), shift(file, X_DOWN)
    half = first_steps(slot_row, piv)
    line_up, file_up, half = lax.optimization_barrier((line_up, file_up, half))
    line = (line, line_up, line_down, shift(line_up, Y_UP))
    file = (file, file_up, file_down, shift(file_up, X_UP))
    inv, inv_rel = last_steps(slot_rel, half)

    own_cb = own_ids >= PIVOTS
    column_iota = jnp.arange(width, dtype=I32)
    own_target = jnp.sum(
        jnp.where((own_ids - PIVOTS)[:, None] == column_iota[None, :], own_map[None, :], 0), axis=1
    )
    owner = jnp.where(own_cb, own_target // parent_rows, -1)
    row_iota = jnp.arange(rows, dtype=I32)
    same = (owner[:, None] == owner[None, :]) & (row_iota[None, :] < row_iota[:, None])
    place = jnp.where(own_cb, owner * cap + jnp.sum(same.astype(I32), axis=1), -1)

    first_columns, lower = lower_factor(own_cb[:, None].astype(I32), inv, inv_rel, front_rows)
    factors, outgoing = eliminate(place[None, :], rank, first_columns, lower, front_rows, line, file)
    received = lax.all_to_all(outgoing, ("front", "helper"), split_axis=0, concat_axis=0, tiled=True)

    below, counts = columns_below(child_map, parent_width)
    source = jnp.where(counts > 0, below, -1.0).astype(I32).reshape(fronts, parent_width)
    start = below[:, :, 0].astype(I32)

    own_parent = me * parent_rows + jnp.arange(parent_rows, dtype=I32)
    column = jnp.sum(
        jnp.where(child_map[:, None, :] == own_parent[None, :, None], column_iota + 1, 0), axis=2
    )
    found = column > 0
    stored = jnp.sum(
        jnp.where(
            row_list[:, None, :] == (column + (PIVOTS - 1))[:, :, None],
            jnp.arange(row_list.shape[1], dtype=I32),
            0,
        ),
        axis=2,
    )
    sender = stored // rows
    ahead = jnp.sum(
        (
            found[:, None, :]
            & (sender[:, :, None] == sender[:, None, :])
            & (stored[:, None, :] < stored[:, :, None])
        ).astype(I32),
        axis=2,
    )
    front_iota = jnp.arange(fronts, dtype=I32)
    slot = jnp.where(found, (front_iota[:, None] * helpers + sender) * cap + ahead, -1)
    put = jnp.any(slot[:, :, None] == jnp.arange(devices * cap, dtype=I32), axis=0).astype(BF16)
    assembled = assemble(start, source, put, received, parent)
    return (factors[None], assembled)


def solution(mesh):
    in_specs = (P("front", "helper", None), P(), P(), P(("front", "helper"), None))
    out_specs = (P("front", "helper", None), P(("front", "helper"), None))
    return jax.shard_map(local, mesh=mesh, in_specs=in_specs, out_specs=out_specs, check_vma=False)
```
